32 devices in a mesh: row: 4 (over y, x), col: 8 (over z, core).
Axes of the slice: x: 2, y: 2, z: 4, core: 2. Of those that a mesh axis runs over, the one named last changes fastest.
Arguments:
- tokens: bfloat16 [4096, 4096], P(('row', 'col')), may hold values from -6 to 6
- expert_ids: int32 [4096, 2], P(('row', 'col')), may hold values from 0 to 7, all different within a row; in each aligned block of 128 rows (0 to 127, 128 to 255, ...) at most 40 rows name the same one
- gate_weights: float32 [4096, 2], P(('row', 'col')), may hold values from 0.1 to 1
- w_gate: bfloat16 [8, 4096, 1536], P('col', None, 'row'), may hold values from -0.09375 to 0.09375
- w_up: bfloat16 [8, 4096, 1536], P('col', None, 'row'), may hold values from -0.09375 to 0.09375
- w_down: bfloat16 [8, 1536, 4096], P('col', None, 'row'), may hold values from -0.15625 to 0.15625
Outputs:
- moe_out: bfloat16 [4096, 4096], P(('row', 'col'))
The draws below stay inside these ranges and needn't reach their ends.
Inputs may be any that keep to these rules, and one draw needn't show every extreme that they name: `expert_ids`: each row names 2 different experts. Among the 128 rows of one device no expert is named by more than 40 rows, and in every draw some expert is named by exactly 40 rows of some device.
All inputs are finite; a program needn't handle non-finite values.
Results may differ from the reference program's by a relative error of at most 0.0058.
Values may be sent and summed in bfloat16 or wider, within the bound.
A program may use at most 128 MiB of HBM per device.

```python
import math
import jax
import jax.numpy as jnp
import numpy as np
from jax import lax

D = 4096
FF = 1536
TOP = 2
TOK_DEV = 128
EXPERTS = 8
CAP = 40
TOKENS = 4096


def level_of(key, extent, split, low, top_value):
    gain, own = 1.0, jax.random.fold_in(key, 6)
    for dim, parts in split:
        draws = jnp.exp(jax.random.uniform(jax.random.fold_in(own, dim), (parts,), jnp.float32, low / len(split), top_value / len(split)))
        gain = gain * jnp.repeat(draws, extent[dim] // parts).reshape([-1 if axis == dim else 1 for axis in range(len(extent))])
    return gain


def deal_out(stream_key, own, number, rows, count, top, bound, lean):
    ranking = jax.random.permutation(stream_key, count)
    heavy_load, ordinary = load_shares(count, rows * top, bound, lean, True), load_shares(count, rows * top, bound, lean, False)
    places = jnp.arange(count)

    def named(tallies, rotation):
        used = int((tallies > 0).sum())
        fixed = max(1, used // 4)
        shifted = fixed + (places - fixed + rotation * (used - fixed)) % max(1, count - fixed)
        return jnp.zeros((count,), jnp.int32).at[ranking[jnp.where(places < fixed, places, shifted)]].set(jnp.asarray(tallies, jnp.int32))

    tallies = jnp.where(number % 4 == 0, named(heavy_load, number // 4), named(ordinary, number - number // 4 - 1))
    mixed = jax.random.permutation(jax.random.fold_in(own, 3), count)
    donor, sink = mixed[0:count // 2 * 2:2], mixed[1:count // 2 * 2:2]
    margin = jnp.minimum(tallies[donor] - 1, bound - tallies[sink]) // 2
    margin = jnp.where((donor == ranking[0]) | (sink == ranking[0]) | (tallies[sink] == 0), 0, jnp.maximum(margin, 0))
    shifted = jax.random.randint(jax.random.fold_in(own, 4), (count // 2,), 0, 1 << 20) % (margin + 1)
    tallies = tallies.at[donor].add(-shifted).at[sink].add(shifted)
    labels = jnp.searchsorted(jnp.cumsum(tallies), jnp.arange(rows * top), side="right").astype(jnp.int32)
    table = labels.reshape(top, rows).T
    table = table[jax.random.permutation(jax.random.fold_in(own, 1), rows)]
    rotation = jax.random.randint(jax.random.fold_in(own, 2), (rows, 1), 0, top)
    return jnp.take_along_axis(table, (jnp.arange(top)[None, :] + rotation) % top, axis=1)


def load_shares(amount, total, bound, slope, full):
    portions = [(1 << 20) // math.isqrt(grade ** slope) + 1 for grade in range(1, amount + 1)]
    largest = bound if full else min(bound, max(-(-total // amount), total * portions[0] // sum(portions)))
    least = 1 if total - largest >= amount - 1 else 0
    holding, spare = [largest] + [least] * (amount - 1), total - largest - least * (amount - 1)
    while spare > 0:
        movable = [i for i in range(1, amount) if holding[i] < largest] or [i for i in range(1, amount) if holding[i] < bound]
        pool, left = sum([portions[i] for i in movable]), spare
        for i in movable:
            addition = min(bound - holding[i], max(1, left * portions[i] // pool), spare)
            holding[i] = holding[i] + addition
            spare = spare - addition
    return np.array(holding)


def normal_values(key, shape, width, reach, shards=(), kind=jnp.bfloat16):
    values = width * jax.random.normal(key, shape, jnp.float32)
    if shards:
        values = values * level_of(key, shape, shards, -0.22, 0.18)
    return jnp.clip(values, -reach, reach).astype(kind)


def setup_inputs(seed: int = 0) -> dict:
    keys = jax.random.split(jax.random.key(seed), 7)
    tokens = normal_values(keys[0], (TOKENS, D), 1.0, 6.0, ((0, 32),))
    expert_ids_keys = jax.random.split(jax.random.fold_in(keys[1], 1), TOKENS // TOK_DEV)
    expert_ids_turns = jax.random.permutation(jax.random.fold_in(keys[1], 3), TOKENS // TOK_DEV)
    expert_ids = jax.vmap(lambda own, number: deal_out(jax.random.fold_in(keys[1], 2), own, number, TOK_DEV, EXPERTS, TOP, CAP, 2))(expert_ids_keys, expert_ids_turns).reshape((TOKENS, TOP))
    gate_weights = jnp.clip(jnp.exp(math.log(1.0) - 2.3025851 * jax.random.uniform(keys[2], (TOKENS, TOP), jnp.float32) ** level_of(keys[2], (TOKENS, TOP), ((0, 32),), -0.2, 0.2)), 0.1, 1.0)
    w_gate = normal_values(keys[3], (EXPERTS, D, FF), D ** -0.5, 0.09375, ((0, 8), (2, 4)))
    w_up = normal_values(keys[4], (EXPERTS, D, FF), D ** -0.5, 0.09375, ((0, 8), (2, 4)))
    w_down = normal_values(keys[5], (EXPERTS, FF, D), FF ** -0.5, 0.15625, ((0, 8), (2, 4)))
    return dict(tokens=tokens, expert_ids=expert_ids, gate_weights=gate_weights, w_gate=w_gate, w_up=w_up, w_down=w_down)


def reference(tokens, expert_ids, gate_weights, w_gate, w_up, w_down):
    devices = TOKENS // TOK_DEV
    flat_ids = expert_ids.reshape(devices, TOK_DEV * TOP)
    onehot = (flat_ids[:, :, None] == jnp.arange(EXPERTS, dtype=jnp.int32)[None, None, :]).astype(jnp.int32)
    earlier = jnp.cumsum(onehot, axis=1) - onehot
    position = jnp.sum(earlier * onehot, axis=2).astype(jnp.int32)
    slot_ids = (jnp.arange(devices, dtype=jnp.int32)[:, None] * CAP + position).astype(jnp.int32)
    token_of = (jnp.arange(TOKENS * TOP, dtype=jnp.int32) // TOP).astype(jnp.int32)
    shares = gate_weights / jnp.sum(gate_weights, axis=1, keepdims=True)
    row_table = jnp.full((EXPERTS, devices * CAP), TOKENS, jnp.int32)
    row_table = row_table.at[flat_ids.reshape(-1), slot_ids.reshape(-1)].set(token_of)
    weight_table = jnp.zeros((EXPERTS, devices * CAP), jnp.float32)
    weight_table = weight_table.at[flat_ids.reshape(-1), slot_ids.reshape(-1)].set(shares.reshape(-1))
    padded = jnp.concatenate([tokens, jnp.zeros((1, D), tokens.dtype)], axis=0)

    def one_expert(total, inputs):
        row_index, weights, gate_matrix, up_matrix, down_matrix = inputs
        rows = padded[row_index]
        gate_part = jnp.dot(rows, gate_matrix, preferred_element_type=jnp.float32)
        up_part = jnp.dot(rows, up_matrix, preferred_element_type=jnp.float32)
        hidden = (jax.nn.silu(gate_part) * up_part).astype(jnp.bfloat16)
        result = jnp.dot(hidden, down_matrix, preferred_element_type=jnp.float32).astype(jnp.bfloat16)
        total = total.at[row_index].add(weights[:, None] * result.astype(jnp.float32))
        return total, None

    start_total = jnp.zeros((TOKENS + 1, D), jnp.float32)
    total, _ = lax.scan(one_expert, start_total, (row_table, weight_table, w_gate, w_up, w_down))
    return total[:TOKENS].astype(jnp.bfloat16)
```

```python
import functools

import jax
import jax.numpy as jnp
from jax import lax
from jax.experimental import pallas as pl
from jax.experimental.pallas import tpu as pltpu
from jax.sharding import PartitionSpec as P

MESH = pl.DeviceIdType.MESH
F32 = jnp.float32
BF16 = jnp.bfloat16


def flip(value, mask):
    bit = 1
    while bit <= mask:
        if mask & bit:
            value = value + bit * (1 - 2 * lax.rem(lax.div(value, bit), 2))
        bit *= 2
    return value


def kernel(
    ids_ref, gate_ref, tok_ref, wg_ref, wu_ref, wd_ref, out_ref,
    outg, rows, w, wd, acc, hid, part, res, pick,
    w_sem, z_send, z_recv, x_send, x_recv, y_send, y_recv, d_send, d_recv,
    h_send, h_recv, r_send, r_recv,
):
    row, col = lax.axis_index("row"), lax.axis_index("col")
    columns, groups, cap, width = rows.shape
    tokens = tok_ref.shape[0]
    units = wg_ref.shape[2]
    quarter = wd_ref.shape[2]
    steps = columns // 2
    slots = columns * cap
    span = 2 * groups * cap

    def peer(k, m):
        return (flip(row, k), flip(col, m))

    barrier = pltpu.get_barrier_semaphore()
    for k in range(groups):
        for m in range(columns):
            if k or m:
                pl.semaphore_signal(barrier, inc=1, device_id=peer(k, m), device_id_type=MESH)

    loads = [
        pltpu.make_async_copy(wg_ref.at[0], w.at[:, pl.ds(0, units)], w_sem.at[0]),
        pltpu.make_async_copy(wu_ref.at[0], w.at[:, pl.ds(units, units)], w_sem.at[1]),
    ]
    for k in range(groups):
        start = pl.multiple_of(flip(row, k) * units, units)
        loads.append(
            pltpu.make_async_copy(wd_ref.at[0, pl.ds(start, units)], wd.at[k], w_sem.at[2 + k])
        )
    for load in loads:
        load.start()

    ids = ids_ref[...]
    block = lax.broadcasted_iota(jnp.int32, (columns, tokens), 0)
    named = [(ids[k : k + 1, :] == block).astype(F32) for k in range(2)]
    before = (
        lax.broadcasted_iota(jnp.int32, (tokens, tokens), 0)
        < lax.broadcasted_iota(jnp.int32, (tokens, tokens), 1)
    ).astype(F32).astype(BF16)
    place = jnp.dot((named[0] + named[1]).astype(BF16), before, preferred_element_type=F32)
    place = place.astype(jnp.int32)
    slot = lax.broadcasted_iota(jnp.int32, (columns, cap, tokens), 1)
    hit = place[:, None, :] == slot
    chosen = [jnp.where(hit, n[:, None, :], 0.0).reshape(slots, tokens) for n in named]
    for k in range(2):
        pick[k] = chosen[k].astype(BF16)
    both = (chosen[0] + chosen[1]).astype(BF16)
    tile = 512
    for j in range(width // tile):
        at = pl.ds(j * tile, tile)
        sent = jnp.dot(both, tok_ref[:, at], preferred_element_type=F32)
        sent = sent.reshape(columns, cap, tile).astype(BF16)
        rows[0, 0, :, at] = sent[0]
        outg[:, :, at] = sent[1:]

    def remote(src, dst, send, recv, k, m):
        return pltpu.make_async_remote_copy(
            src_ref=src, dst_ref=dst, send_sem=send, recv_sem=recv,
            device_id=peer(k, m), device_id_type=MESH,
        )

    zc = {
        m: remote(outg.at[m - 1], rows.at[m, 0], z_send.at[m - 1], z_recv.at[m - 1], 0, m)
        for m in range(1, columns)
    }
    xc = [remote(rows.at[m, 0], rows.at[m, 1], x_send.at[m], x_recv.at[m], 1, 0) for m in range(columns)]
    yc = [remote(rows.at[m, 0], rows.at[m, 2], y_send.at[m], y_recv.at[m], 2, 0) for m in range(columns)]
    dc = [
        remote(rows.at[m, 1 + m % 2], rows.at[m, 3], d_send.at[m], d_recv.at[m], 2 - m % 2, 0)
        for m in range(columns)
    ]
    hx = [remote(hid.at[0, g], hid.at[1, g], h_send.at[g, 0], h_recv.at[g, 0], 1, 0) for g in range(steps)]
    hy = [remote(hid.at[0, g], hid.at[2, g], h_send.at[g, 1], h_recv.at[g, 1], 2, 0) for g in range(steps)]
    hd = [
        remote(hid.at[1 + g % 2, g], hid.at[3, g], h_send.at[g, 2], h_recv.at[g, 2], 2 - g % 2, 0)
        for g in range(steps)
    ]
    rc = {
        (m, k): remote(part.at[m, k], res.at[k, m], r_send.at[m, k], r_recv.at[m, k], k, m)
        for m in range(columns) for k in range(groups) if k or m
    }

    pl.semaphore_wait(barrier, groups * columns - 1)

    def stage_a(g):
        for m in (2 * g, 2 * g + 1):
            if m:
                zc[m].wait_recv()
            xc[m].start()
            yc[m].start()

    def stage_b(g):
        for m in (2 * g, 2 * g + 1):
            xc[m].wait_recv()
            yc[m].wait_recv()
            dc[m].start()

    def stage_c(g):
        for m in (2 * g, 2 * g + 1):
            dc[m].wait_recv()
        if g == 0:
            loads[0].wait()
            loads[1].wait()
        acc[...] = jnp.zeros_like(acc)
        depth = 512

        def body(i, carry):
            at = pl.ds(pl.multiple_of(i * depth, depth), depth)
            lhs = rows[2 * g : 2 * g + 2, :, :, at].reshape(span, depth)
            acc[...] += jnp.dot(lhs, w[at, :], preferred_element_type=F32)
            return carry

        lax.fori_loop(0, width // depth, body, 0)
        gate, up = acc[:, :units], acc[:, units:]
        hid[0, g] = (gate / (1.0 + jnp.exp(-gate)) * up).astype(BF16)
        hx[g].start()
        hy[g].start()

    def stage_d(g):
        hx[g].wait_recv()
        hy[g].wait_recv()
        hd[g].start()

    def stage_e(g):
        hd[g].wait_recv()
        if g == 0:
            for load in loads[2:]:
                load.wait()
        wide = 256

        def body(i, carry):
            at = pl.ds(pl.multiple_of(i * wide, wide), wide)
            total = [None] * groups
            for q in range(groups):
                out = jnp.dot(hid[q, g], wd[q, :, at], preferred_element_type=F32)
                out = out.reshape(2, groups, cap, wide)
                for k in range(groups):
                    term = out[:, k]
                    total[k ^ q] = term if total[k ^ q] is None else total[k ^ q] + term
            for k in range(groups):
                part[2 * g : 2 * g + 2, k, :, at] = total[k].astype(BF16)
            if g == 0:
                res[0, 0, :, at] = total[0][0].astype(BF16)
            return carry

        lax.fori_loop(0, quarter // wide, body, 0)
        for m in (2 * g, 2 * g + 1):
            for k in range(groups):
                if k or m:
                    rc[m, k].start()

    for m in range(1, columns):
        zc[m].start()
    for turn in range(steps + 4):
        for offset, stage in enumerate((stage_a, stage_b, stage_c, stage_d, stage_e)):
            if 0 <= turn - offset < steps:
                stage(turn - offset)

    share = gate_ref[...]
    share = share / jnp.sum(share, axis=1, keepdims=True)
    for copy in rc.values():
        copy.wait_recv()
    for k in range(groups):
        got = res[k].reshape(slots, quarter)
        total = None
        for choice in range(2):
            term = lax.dot_general(
                pick[choice], got, (((0,), (0,)), ((), ())), preferred_element_type=F32
            )
            term = share[:, choice : choice + 1] * term
            total = term if total is None else total + term
        at = pl.ds(pl.multiple_of(flip(row, k) * quarter, quarter), quarter)
        out_ref[:, at] = total.astype(BF16)

    for copy in [*zc.values(), *xc, *yc, *dc, *hx, *hy, *hd, *rc.values()]:
        copy.wait_send()


def fused(tokens, expert_ids, gate_weights, w_gate, w_up, w_down, cap):
    columns, groups = lax.axis_size("col"), lax.axis_size("row")
    count, width = tokens.shape
    units, quarter = w_gate.shape[2], w_down.shape[2]
    ids = expert_ids.T ^ lax.axis_index("col")
    dma = pltpu.SemaphoreType.DMA
    vmem = pl.BlockSpec(memory_space=pltpu.VMEM)
    hbm = pl.BlockSpec(memory_space=pl.ANY)
    slots = columns * cap
    return pl.pallas_call(
        kernel,
        out_shape=jax.ShapeDtypeStruct((count, width), BF16),
        in_specs=[vmem] * 3 + [hbm] * 3,
        out_specs=vmem,
        scratch_shapes=[
            pltpu.VMEM((columns - 1, cap, width), BF16),
            pltpu.VMEM((columns, groups, cap, width), BF16),
            pltpu.VMEM((width, 2 * units), BF16),
            pltpu.VMEM((groups, units, quarter), BF16),
            pltpu.VMEM((2 * groups * cap, 2 * units), F32),
            pltpu.VMEM((groups, columns // 2, 2 * groups * cap, units), BF16),
            pltpu.VMEM((columns, groups, cap, quarter), BF16),
            pltpu.VMEM((groups, columns, cap, quarter), BF16),
            pltpu.VMEM((2, slots, count), BF16),
            dma((2 + groups,)),
            dma((columns - 1,)), dma((columns - 1,)),
            dma((columns,)), dma((columns,)),
            dma((columns,)), dma((columns,)),
            dma((columns,)), dma((columns,)),
            dma((columns // 2, 3)), dma((columns // 2, 3)),
            dma((columns, groups)), dma((columns, groups)),
        ],
        compiler_params=pltpu.CompilerParams(
            collective_id=0, has_side_effects=True, vmem_limit_bytes=60 * 2**20
        ),
        cost_estimate=pl.CostEstimate(
            flops=2 * slots * groups * width * units * 3, bytes_accessed=12 * 2**20, transcendentals=0
        ),
    )(ids, gate_weights, tokens, w_gate, w_up, w_down)


def local(tokens, expert_ids, gate_weights, w_gate, w_up, w_down):
    token_count, top_count = expert_ids.shape
    width = tokens.shape[1]
    local_count = w_gate.shape[0]
    unit_count = w_gate.shape[2]
    quarter = w_down.shape[2]
    columns = lax.axis_size("col")
    groups = lax.axis_size("row")
    experts = local_count * columns
    capacity = max(2, token_count * top_count * 5 // (4 * experts))
    if groups == 4 and columns == 8 and local_count == 1 and top_count == 2 and capacity % 8 == 0:
        return fused(tokens, expert_ids, gate_weights, w_gate, w_up, w_down, capacity)
    flat_ids = expert_ids.reshape(-1)
    onehot = (flat_ids[:, None] == jnp.arange(experts, dtype=jnp.int32)[None, :]).astype(jnp.int32)
    entries = jnp.arange(flat_ids.shape[0], dtype=jnp.int32)
    before = (entries[None, :] < entries[:, None]).astype(jnp.bfloat16)
    earlier = jnp.dot(before, onehot.astype(jnp.bfloat16), preferred_element_type=jnp.float32).astype(jnp.int32)
    position = jnp.sum(earlier * onehot, axis=1)
    slot_ids = (flat_ids * capacity + position).reshape(token_count, top_count)
    chooser = jnp.any(
        jnp.arange(experts * capacity, dtype=jnp.int32)[:, None, None] == slot_ids[None, :, :],
        axis=2,
    ).astype(jnp.bfloat16)
    outgoing = jnp.dot(chooser, tokens, preferred_element_type=jnp.float32).astype(jnp.bfloat16)
    outgoing = outgoing.reshape(columns, local_count * capacity, width)
    arrived = lax.all_to_all(outgoing, "col", split_axis=0, concat_axis=0, tiled=True)
    block_rows = lax.all_gather(arrived[None], "row", axis=0, tiled=True)
    count = block_rows.shape[0]
    grouped = block_rows.reshape(count, columns, local_count, capacity, width)
    expert = 0
    inputs = grouped[:, :, expert].reshape(-1, width)
    gate_part = jnp.dot(inputs, w_gate[expert], preferred_element_type=jnp.float32)
    up_part = jnp.dot(inputs, w_up[expert], preferred_element_type=jnp.float32)
    hidden = (jax.nn.silu(gate_part) * up_part).astype(jnp.bfloat16)
    outputs = hidden.reshape(count, columns, 1, capacity, unit_count)
    hidden_all = outputs.reshape(count, columns, local_count * capacity, unit_count)
    hidden_split = hidden_all.reshape(groups, columns, local_count, capacity, unit_count)
    piece = lax.all_gather(hidden_split, "row", axis=4, tiled=True)
    count = piece.shape[4]
    expert = 0
    rows = piece[:, :, expert].reshape(-1, count)
    block = w_down[expert]
    parts = [jnp.dot(rows, block, preferred_element_type=jnp.float32)]
    summed = jnp.stack(parts)
    expert_out = summed.astype(jnp.bfloat16).reshape(
        local_count, groups, columns, capacity, quarter
    )
    expert_out = jnp.transpose(expert_out, (1, 2, 0, 3, 4)).reshape(
        groups, columns, local_count * capacity, quarter
    )
    colwise = lax.all_to_all(expert_out, "col", split_axis=1, concat_axis=1, tiled=True)
    home = lax.all_to_all(colwise, "row", split_axis=0, concat_axis=3, tiled=True)
    results = home.reshape(experts * capacity, width)
    shares = gate_weights / jnp.sum(gate_weights, axis=1, keepdims=True)
    picked = results[slot_ids].astype(jnp.float32)
    combined = jnp.sum(shares[:, :, None] * picked, axis=1)
    return combined.astype(jnp.bfloat16)


def solution(mesh):
    placed = (
        P(("row", "col"), None),
        P(("row", "col"), None),
        P(("row", "col"), None),
        P("col", None, "row"),
        P("col", None, "row"),
        P("col", None, "row"),
    )
    return jax.shard_map(
        local, mesh=mesh, in_specs=placed, out_specs=P(("row", "col"), None), check_vma=False
    )
```

```python
import functools

import jax
import jax.numpy as jnp
from jax import lax
from jax.experimental import pallas as pl
from jax.experimental.pallas import tpu as pltpu
from jax.sharding import PartitionSpec as P

MESH = pl.DeviceIdType.MESH
ORDER = (0, 1, 2, 3, 4, 5, 6, 7)
SIZES = (1,)*8
LAGS = (0, 1, 2, 3, 4)
NEWEST_FIRST = False
AHEAD = 99
F32 = jnp.float32
BF16 = jnp.bfloat16


def flip(value, mask):
    bit = 1
    while bit <= mask:
        if mask & bit:
            value = value + bit * (1 - 2 * lax.rem(lax.div(value, bit), 2))
        bit *= 2
    return value


def kernel(
    ids_ref, gate_ref, tok_ref, wg_ref, wu_ref, wd_ref, out_ref,
    outg, rows, w, wd, acc, hid, part, res, pick,
    w_sem, z_send, z_recv, x_send, x_recv, y_send, y_recv, d_send, d_recv,
    h_send, h_recv, r_send, r_recv,
):
    row, col = lax.axis_index("row"), lax.axis_index("col")
    columns, groups, cap, width = rows.shape
    tokens = tok_ref.shape[0]
    units = wg_ref.shape[2]
    quarter = wd_ref.shape[2]
    steps = len(SIZES)
    firsts = [sum(SIZES[:g]) for g in range(steps)]
    slots = columns * cap

    def peer(k, m):
        return (flip(row, k), flip(col, m))

    barrier = pltpu.get_barrier_semaphore()
    for k in range(groups):
        for m in range(columns):
            if k or m:
                pl.semaphore_signal(barrier, inc=1, device_id=peer(k, m), device_id_type=MESH)

    loads = [
        pltpu.make_async_copy(wg_ref.at[0], w.at[:, pl.ds(0, units)], w_sem.at[0]),
        pltpu.make_async_copy(wu_ref.at[0], w.at[:, pl.ds(units, units)], w_sem.at[1]),
    ]
    for k in range(groups):
        start = pl.multiple_of(flip(row, k) * units, units)
        loads.append(
            pltpu.make_async_copy(wd_ref.at[0, pl.ds(start, units)], wd.at[k], w_sem.at[2 + k])
        )
    for load in loads:
        load.start()

    ids = ids_ref[...]
    block = lax.broadcasted_iota(jnp.int32, (columns, tokens), 0)
    masks = jnp.zeros_like(block)
    for p, m in enumerate(ORDER):
        masks = jnp.where(block == p, m, masks)
    named = [(ids[k : k + 1, :] == masks).astype(F32) for k in range(2)]
    before = (
        lax.broadcasted_iota(jnp.int32, (tokens, tokens), 0)
        < lax.broadcasted_iota(jnp.int32, (tokens, tokens), 1)
    ).astype(F32).astype(BF16)
    place = jnp.dot((named[0] + named[1]).astype(BF16), before, preferred_element_type=F32)
    place = place.astype(jnp.int32)
    slot = lax.broadcasted_iota(jnp.int32, (columns, cap, tokens), 1)
    hit = place[:, None, :] == slot
    chosen = [jnp.where(hit, n[:, None, :], 0.0).reshape(slots, tokens) for n in named]
    for k in range(2):
        pick[k] = chosen[k].astype(BF16)
    both = (chosen[0] + chosen[1]).astype(BF16)
    tile = 512
    for j in range(width // tile):
        at = pl.ds(j * tile, tile)
        sent = jnp.dot(both, tok_ref[:, at], preferred_element_type=F32)
        sent = sent.reshape(columns, cap, tile).astype(BF16)
        rows[0, 0, :, at] = sent[0]
        outg[:, :, at] = sent[1:]

    def remote(src, dst, send, recv, k, m):
        return pltpu.make_async_remote_copy(
            src_ref=src, dst_ref=dst, send_sem=send, recv_sem=recv,
            device_id=peer(k, m), device_id_type=MESH,
        )

    zc = {
        m: remote(outg.at[m - 1], rows.at[m, 0], z_send.at[m - 1], z_recv.at[m - 1], 0, ORDER[m])
        for m in range(1, columns)
    }
    xc = [remote(rows.at[m, 0], rows.at[m, 1], x_send.at[m], x_recv.at[m], 1, 0) for m in range(columns)]
    yc = [remote(rows.at[m, 0], rows.at[m, 2], y_send.at[m], y_recv.at[m], 2, 0) for m in range(columns)]
    dc = [
        remote(rows.at[m, 1 + m % 2], rows.at[m, 3], d_send.at[m], d_recv.at[m], 2 - m % 2, 0)
        for m in range(columns)
    ]

    def units_copy(g, source, target, number, k):
        at = pl.ds(firsts[g], SIZES[g])
        return remote(
            hid.at[source, at], hid.at[target, at], h_send.at[g, number], h_recv.at[g, number], k, 0
        )

    hx = [units_copy(g, 0, 1, 0, 1) for g in range(steps)]
    hy = [units_copy(g, 0, 2, 1, 2) for g in range(steps)]
    hd = [units_copy(g, 1 + g % 2, 3, 2, 2 - g % 2) for g in range(steps)]
    rc = {
        (m, k): remote(part.at[m, k], res.at[k, m], r_send.at[m, k], r_recv.at[m, k], k, ORDER[m])
        for m in range(columns) for k in range(groups) if k or m
    }

    pl.semaphore_wait(barrier, groups * columns - 1)

    def stage_a(g):
        for m in range(firsts[g], firsts[g] + SIZES[g]):
            if m:
                zc[m].wait_recv()
            xc[m].start()
            yc[m].start()

    def stage_b(g):
        for m in range(firsts[g], firsts[g] + SIZES[g]):
            xc[m].wait_recv()
            yc[m].wait_recv()
            dc[m].start()

    def stage_c(g):
        for m in range(firsts[g], firsts[g] + SIZES[g]):
            dc[m].wait_recv()
        if g == 0:
            loads[0].wait()
            loads[1].wait()
        span = SIZES[g] * groups * cap
        acc[:span] = jnp.zeros((span, 2 * units), F32)
        depth = 512

        def body(i, carry):
            at = pl.ds(pl.multiple_of(i * depth, depth), depth)
            lhs = rows[firsts[g] : firsts[g] + SIZES[g], :, :, at].reshape(span, depth)
            acc[:span] += jnp.dot(lhs, w[at, :], preferred_element_type=F32)
            return carry

        lax.fori_loop(0, width // depth, body, 0)
        gate, up = acc[:span, :units], acc[:span, units:]
        value = (gate / (1.0 + jnp.exp(-gate)) * up).astype(BF16)
        hid[0, firsts[g] : firsts[g] + SIZES[g]] = value.reshape(SIZES[g], groups * cap, units)
        hx[g].start()
        hy[g].start()

    def stage_d(g):
        hx[g].wait_recv()
        hy[g].wait_recv()
        hd[g].start()

    def stage_e(g):
        hd[g].wait_recv()
        if g == 0:
            for load in loads[2:]:
                load.wait()
        wide = 256

        def body(i, carry):
            at = pl.ds(pl.multiple_of(i * wide, wide), wide)
            total = [None] * groups
            for q in range(groups):
                left = hid[q, firsts[g] : firsts[g] + SIZES[g]].reshape(-1, units)
                out = jnp.dot(left, wd[q, :, at], preferred_element_type=F32)
                out = out.reshape(SIZES[g], groups, cap, wide)
                for k in range(groups):
                    term = out[:, k]
                    total[k ^ q] = term if total[k ^ q] is None else total[k ^ q] + term
            for k in range(groups):
                part[firsts[g] : firsts[g] + SIZES[g], k, :, at] = total[k].astype(BF16)
            if g == 0:
                res[0, 0, :, at] = total[0][0].astype(BF16)
            return carry

        lax.fori_loop(0, quarter // wide, body, 0)
        for m in range(firsts[g], firsts[g] + SIZES[g]):
            for k in range(groups):
                if k or m:
                    rc[m, k].start()

    stages = list(enumerate((stage_a, stage_b, stage_c, stage_d, stage_e)))
    if not NEWEST_FIRST:
        stages.reverse()
    begun = 1
    for turn in range(steps + LAGS[-1]):
        while begun < columns and begun < sum(SIZES[: turn + 1 + AHEAD]):
            zc[begun].start()
            begun += 1
        for number, stage in stages:
            if 0 <= turn - LAGS[number] < steps:
                stage(turn - LAGS[number])

    share = gate_ref[...]
    share = share / jnp.sum(share, axis=1, keepdims=True)
    for copy in rc.values():
        copy.wait_recv()
    for k in range(groups):
        got = res[k].reshape(slots, quarter)
        total = None
        for choice in range(2):
            term = lax.dot_general(
                pick[choice], got, (((0,), (0,)), ((), ())), preferred_element_type=F32
            )
            term = share[:, choice : choice + 1] * term
            total = term if total is None else total + term
        at = pl.ds(pl.multiple_of(flip(row, k) * quarter, quarter), quarter)
        out_ref[:, at] = total.astype(BF16)

    for copy in [*zc.values(), *xc, *yc, *dc, *hx, *hy, *hd, *rc.values()]:
        copy.wait_send()


def fused(tokens, expert_ids, gate_weights, w_gate, w_up, w_down, cap):
    columns, groups = lax.axis_size("col"), lax.axis_size("row")
    count, width = tokens.shape
    units, quarter = w_gate.shape[2], w_down.shape[2]
    ids = expert_ids.T ^ lax.axis_index("col")
    dma = pltpu.SemaphoreType.DMA
    vmem = pl.BlockSpec(memory_space=pltpu.VMEM)
    hbm = pl.BlockSpec(memory_space=pl.ANY)
    slots = columns * cap
    return pl.pallas_call(
        kernel,
        out_shape=jax.ShapeDtypeStruct((count, width), BF16),
        in_specs=[vmem] * 3 + [hbm] * 3,
        out_specs=vmem,
        scratch_shapes=[
            pltpu.VMEM((columns - 1, cap, width), BF16),
            pltpu.VMEM((columns, groups, cap, width), BF16),
            pltpu.VMEM((width, 2 * units), BF16),
            pltpu.VMEM((groups, units, quarter), BF16),
            pltpu.VMEM((max(SIZES) * groups * cap, 2 * units), F32),
            pltpu.VMEM((groups, columns, groups * cap, units), BF16),
            pltpu.VMEM((columns, groups, cap, quarter), BF16),
            pltpu.VMEM((groups, columns, cap, quarter), BF16),
            pltpu.VMEM((2, slots, count), BF16),
            dma((2 + groups,)),
            dma((columns - 1,)), dma((columns - 1,)),
            dma((columns,)), dma((columns,)),
            dma((columns,)), dma((columns,)),
            dma((columns,)), dma((columns,)),
            dma((len(SIZES), 3)), dma((len(SIZES), 3)),
            dma((columns, groups)), dma((columns, groups)),
        ],
        compiler_params=pltpu.CompilerParams(
            collective_id=0, has_side_effects=True, vmem_limit_bytes=60 * 2**20
        ),
        cost_estimate=pl.CostEstimate(
            flops=2 * slots * groups * width * units * 3, bytes_accessed=12 * 2**20, transcendentals=0
        ),
    )(ids, gate_weights, tokens, w_gate, w_up, w_down)


def local(tokens, expert_ids, gate_weights, w_gate, w_up, w_down):
    token_count, top_count = expert_ids.shape
    width = tokens.shape[1]
    local_count = w_gate.shape[0]
    unit_count = w_gate.shape[2]
    quarter = w_down.shape[2]
    columns = lax.axis_size("col")
    groups = lax.axis_size("row")
    experts = local_count * columns
    capacity = max(2, token_count * top_count * 5 // (4 * experts))
    if groups == 4 and columns == 8 and local_count == 1 and top_count == 2 and capacity % 8 == 0:
        return fused(tokens, expert_ids, gate_weights, w_gate, w_up, w_down, capacity)
    flat_ids = expert_ids.reshape(-1)
    onehot = (flat_ids[:, None] == jnp.arange(experts, dtype=jnp.int32)[None, :]).astype(jnp.int32)
    entries = jnp.arange(flat_ids.shape[0], dtype=jnp.int32)
    before = (entries[None, :] < entries[:, None]).astype(jnp.bfloat16)
    earlier = jnp.dot(before, onehot.astype(jnp.bfloat16), preferred_element_type=jnp.float32).astype(jnp.int32)
    position = jnp.sum(earlier * onehot, axis=1)
    slot_ids = (flat_ids * capacity + position).reshape(token_count, top_count)
    chooser = jnp.any(
        jnp.arange(experts * capacity, dtype=jnp.int32)[:, None, None] == slot_ids[None, :, :],
        axis=2,
    ).astype(jnp.bfloat16)
    outgoing = jnp.dot(chooser, tokens, preferred_element_type=jnp.float32).astype(jnp.bfloat16)
    outgoing = outgoing.reshape(columns, local_count * capacity, width)
    arrived = lax.all_to_all(outgoing, "col", split_axis=0, concat_axis=0, tiled=True)
    block_rows = lax.all_gather(arrived[None], "row", axis=0, tiled=True)
    count = block_rows.shape[0]
    grouped = block_rows.reshape(count, columns, local_count, capacity, width)
    expert = 0
    inputs = grouped[:, :, expert].reshape(-1, width)
    gate_part = jnp.dot(inputs, w_gate[expert], preferred_element_type=jnp.float32)
    up_part = jnp.dot(inputs, w_up[expert], preferred_element_type=jnp.float32)
    hidden = (jax.nn.silu(gate_part) * up_part).astype(jnp.bfloat16)
    outputs = hidden.reshape(count, columns, 1, capacity, unit_count)
    hidden_all = outputs.reshape(count, columns, local_count * capacity, unit_count)
    hidden_split = hidden_all.reshape(groups, columns, local_count, capacity, unit_count)
    piece = lax.all_gather(hidden_split, "row", axis=4, tiled=True)
    count = piece.shape[4]
    expert = 0
    rows = piece[:, :, expert].reshape(-1, count)
    block = w_down[expert]
    parts = [jnp.dot(rows, block, preferred_element_type=jnp.float32)]
    summed = jnp.stack(parts)
    expert_out = summed.astype(jnp.bfloat16).reshape(
        local_count, groups, columns, capacity, quarter
    )
    expert_out = jnp.transpose(expert_out, (1, 2, 0, 3, 4)).reshape(
        groups, columns, local_count * capacity, quarter
    )
    colwise = lax.all_to_all(expert_out, "col", split_axis=1, concat_axis=1, tiled=True)
    home = lax.all_to_all(colwise, "row", split_axis=0, concat_axis=3, tiled=True)
    results = home.reshape(experts * capacity, width)
    shares = gate_weights / jnp.sum(gate_weights, axis=1, keepdims=True)
    picked = results[slot_ids].astype(jnp.float32)
    combined = jnp.sum(shares[:, :, None] * picked, axis=1)
    return combined.astype(jnp.bfloat16)


def solution(mesh):
    placed = (
        P(("row", "col"), None),
        P(("row", "col"), None),
        P(("row", "col"), None),
        P("col", None, "row"),
        P("col", None, "row"),
        P("col", None, "row"),
    )
    return jax.shard_map(
        local, mesh=mesh, in_specs=placed, out_specs=P(("row", "col"), None), check_vma=False
    )
```
